768 devices in a mesh: row: 16 (over y, x_hi), col: 48 (over z, x_lo, core).
Axes of the slice: x: 4 (x_hi: 2, x_lo: 2; x = x_hi * 2 + x_lo), y: 8, z: 12, core: 2. Of those that a mesh axis runs over, the one named last changes fastest.
Arguments:
- counts: int32 [12288, 24576], P('row', 'col'), may hold values from 0 to 1024, as said below
- item_vec: float32 [12288, 512], P(('row', 'col')), may hold values from -1.2 to 1.2
- item_bias: float32 [12288], P(('row', 'col')), may hold values from -6 to 6
- item_hist: float32 [12288, 512], P(('row', 'col')), may hold values from 0.1 to 1
- context_vec: float32 [24576, 512], P(('col', 'row')), may hold values from -1.2 to 1.2
- context_bias: float32 [24576], P(('col', 'row')), may hold values from -6 to 6
- context_hist: float32 [24576, 512], P(('col', 'row')), may hold values from 0.1 to 1
Outputs:
- item_new: float32 [12288, 512], P(('row', 'col'))
- item_bias_new: float32 [12288], P(('row', 'col'))
- item_hist_new: float32 [12288, 512], P(('row', 'col'))
- context_new: float32 [24576, 512], P(('col', 'row'))
- context_bias_new: float32 [24576], P(('col', 'row'))
- context_hist_new: float32 [24576, 512], P(('col', 'row'))
The draws below stay inside these ranges and needn't reach their ends.
Inputs may be any that keep to these rules, and one draw needn't show every extreme that they name: `counts`: every aligned 128 x 128 tile either has nonzero entries or is all zero; how many tiles are all zero differs between blocks.
All inputs are finite; a program needn't handle non-finite values.
Results may differ from the reference program's by a relative error of at most 0.0029.
Values may be sent and summed in bfloat16 or wider, within the bound.
No kernel may reach another device: no remote copies, remote signals or barrier semaphores. Data moves between devices by JAX's collectives and lax.ppermute only.
A program may use at most 32 MiB of HBM per device.

```python
import math
import jax
import jax.numpy as jnp
from jax import lax

E = 512
TILE = 128
ITEM_BLOCK = 768
CONTEXT_BLOCK = 512
NI = 12288
NJ = 24576
N_ROW = 16
N_COL = 48


def draw_counts(key, part):
    key = jax.random.fold_in(key, 11)
    keys = jax.random.split(key, 6)
    dense_pick = jax.random.randint(keys[0], (N_ROW, N_COL), 0, 4)
    sparse_level = jax.random.randint(keys[1], (N_ROW, N_COL), 1, 4)
    level = jnp.where(dense_pick == 0, 8, sparse_level)
    level_tiles = jnp.repeat(jnp.repeat(level, ITEM_BLOCK // TILE, axis=0), CONTEXT_BLOCK // TILE, axis=1)
    tile_draw = jax.random.randint(keys[2], (NI // TILE, NJ // TILE), 0, 8)
    live_tiles = tile_draw < level_tiles
    live_cells = jnp.repeat(jnp.repeat(live_tiles, TILE, axis=0), TILE, axis=1)
    magnitude = jax.random.randint(keys[3], (NI, NJ), 0, 11)
    base_value = jax.random.randint(keys[4], (NI, NJ), 0, 1024)
    value = base_value // jnp.left_shift(1, 10 - magnitude) + 1
    present = jax.random.randint(keys[5], (NI, NJ), 0, 3) > 0
    counts = jnp.where(live_cells & present, value, 0).astype(jnp.int32)
    return counts.at[0, 0].set(1024)


def steps_of(own_key, extent, cuts, low, high):
    factor_of = 1.0
    for position, blocks in cuts:
        draws = jax.random.uniform(jax.random.fold_in(jax.random.fold_in(own_key, 6), position), (blocks,), jnp.float32, low / len(cuts), high / len(cuts))
        factor_of = factor_of * jnp.repeat(jnp.exp(draws), extent[position] // blocks).reshape((-1,) + (1,) * (len(extent) - 1 - position))
    return factor_of


def normal_values(stream_key, extent, spread, bound, cuts=(), kind=jnp.bfloat16):
    entries = jax.random.normal(stream_key, extent, jnp.float32) * spread
    if len(cuts) > 0:
        entries = steps_of(stream_key, extent, cuts, -0.22, 0.18) * entries
    return jnp.clip(entries, min=-bound, max=bound).astype(kind)


def setup_inputs(seed: int = 0) -> dict:
    key_list = jax.random.split(jax.random.key(seed), 8)
    counts = draw_counts(jax.random.fold_in(key_list[7], 71), 0)
    item_vec = normal_values(key_list[1], (NI, E), 0.2, 1.2, ((0, 768),), jnp.float32)
    item_bias = normal_values(key_list[2], (NI,), 1.0, 6.0, ((0, 768),), jnp.float32)
    item_hist = jnp.clip(jnp.exp(math.log(1.0) - 2.3025851 * jax.random.uniform(key_list[3], (NI, E), jnp.float32) ** steps_of(key_list[3], (NI, E), ((0, 768),), -0.2, 0.2)), 0.1, 1.0)
    context_vec = normal_values(key_list[4], (NJ, E), 0.2, 1.2, ((0, 768),), jnp.float32)
    context_bias = normal_values(key_list[5], (NJ,), 1.0, 6.0, ((0, 768),), jnp.float32)
    context_hist = jnp.clip(jnp.exp(math.log(1.0) - 2.3025851 * jax.random.uniform(key_list[6], (NJ, E), jnp.float32) ** steps_of(key_list[6], (NJ, E), ((0, 768),), -0.2, 0.2)), 0.1, 1.0)
    return dict(counts=counts, item_vec=item_vec, item_bias=item_bias, item_hist=item_hist, context_vec=context_vec, context_bias=context_bias, context_hist=context_hist)


def half_round(values):
    return lax.optimization_barrier(values.astype(jnp.bfloat16)).astype(jnp.float32)

def adagrad(params, history, grad):
    history_new = history + grad * grad
    return (params - 0.2 * grad / jnp.sqrt(history_new), history_new)

def reference(counts, item_vec, item_bias, item_hist, context_vec, context_bias, context_hist):
    item_emb = half_round(item_vec)
    item_off = half_round(item_bias)
    context_emb = half_round(context_vec)
    context_off = half_round(context_bias)
    item_blocks = item_emb.reshape(N_ROW, ITEM_BLOCK, E)
    item_offs = item_off.reshape(N_ROW, ITEM_BLOCK)
    count_blocks = counts.reshape(N_ROW, ITEM_BLOCK, NJ)

    def one_block(running, inputs):
        context_sum, context_bias_sum = running
        block_emb, block_off, block_counts = inputs
        scores = jnp.dot(block_emb, context_emb.T)
        count_float = block_counts.astype(jnp.float32)
        weight = jnp.where(block_counts > 0, jnp.minimum((count_float / 100.0) ** 0.75, 1.0), 0.0)
        mismatch = scores + block_off[:, None] + context_off[None, :] - jnp.log(jnp.maximum(count_float, 1.0))
        resid = half_round(weight * mismatch)
        item_part = jnp.dot(resid, context_emb)
        item_bias_part = lax.optimization_barrier(jnp.sum(resid, axis=1))
        context_sum = context_sum + jnp.dot(resid.T, block_emb)
        context_bias_sum = context_bias_sum + lax.optimization_barrier(jnp.sum(resid, axis=0))
        return ((context_sum, context_bias_sum), (item_part, item_bias_part))
    start = (jnp.zeros((NJ, E), jnp.float32), jnp.zeros((NJ,), jnp.float32))
    (context_sum, context_bias_sum), (item_parts, item_bias_parts) = lax.scan(one_block, start, (item_blocks, item_offs, count_blocks))
    item_grad = item_parts.reshape(NI, E) / math.sqrt(NJ)
    item_bias_grad = item_bias_parts.reshape(NI) / math.sqrt(NJ)
    context_grad = context_sum / math.sqrt(NI)
    context_bias_grad = context_bias_sum / math.sqrt(NI)
    item_new, item_hist_new = adagrad(item_vec, item_hist, item_grad)
    context_new, context_hist_new = adagrad(context_vec, context_hist, context_grad)
    item_bias_new = item_bias - 0.1 * item_bias_grad
    context_bias_new = context_bias - 0.1 * context_bias_grad
    return (item_new, item_bias_new, item_hist_new, context_new, context_bias_new, context_hist_new)
```

```python
import math

import jax
import jax.numpy as jnp
from jax import lax
from jax.sharding import Mesh, PartitionSpec as P

SUB_AXES = ("y", "xh", "z", "xl", "c")
SUB_SIZES = (8, 2, 12, 2, 2)
ROW = ("y", "xh")
COL = ("z", "xl", "c")
SWAP = [(0, 1), (1, 0)]
BF16 = jnp.bfloat16
F32 = jnp.float32
PAD = 128


def adagrad(params, history, grad):
    history_new = history + grad * grad
    return (params - 0.2 * grad / jnp.sqrt(history_new), history_new)


def packed(vec, first, second):
    rows = vec.shape[0]
    pad = jnp.zeros((rows, PAD - 2), BF16)
    return jnp.concatenate([vec.astype(BF16), first[:, None], second[:, None], pad], axis=1)


def pick(array, index, axis):
    return lax.dynamic_index_in_dim(array, index, axis, keepdims=False)


def shards(counts, item_vec, item_bias, item_hist, context_vec, context_bias, context_hist):
    xl = lax.axis_index("xl")
    core = lax.axis_index("c")
    rows_i, width = item_vec.shape
    rows_c = context_vec.shape[0]
    n_row = lax.axis_size(ROW)
    n_z = lax.axis_size("z")
    block_i, block_c = counts.shape
    full = width + PAD

    item_pack = packed(item_vec, item_bias.astype(BF16), jnp.ones((rows_i,), BF16))
    context_pack = packed(context_vec, jnp.ones((rows_c,), BF16), context_bias.astype(BF16))
    item_other = lax.ppermute(item_pack, "xl", SWAP)
    item_pair = jnp.where(
        xl == 0,
        jnp.stack([item_pack, item_other]),
        jnp.stack([item_other, item_pack]),
    )
    context_all = lax.all_to_all(
        jnp.broadcast_to(context_pack[None], (n_row, rows_c, full)), ROW, split_axis=0, concat_axis=0
    ).reshape(block_c, full)
    item_z = lax.all_gather(item_pair, "z", axis=0, tiled=False)
    item_all = lax.all_gather(item_z, "c", axis=2, tiled=False).reshape(block_i, full)

    scores = lax.dot_general(
        item_all, context_all, (((1,), (1,)), ((), ())), preferred_element_type=F32
    )
    count_float = counts.astype(F32)
    weight = jnp.where(counts > 0, jnp.minimum((count_float / 100.0) ** 0.75, 1.0), 0.0)
    resid = (weight * (scores - jnp.log(jnp.maximum(count_float, 1.0)))).astype(BF16)

    context_part = lax.dot_general(
        resid, item_all, (((0,), (0,)), ((), ())), preferred_element_type=F32
    ).astype(BF16)
    context_parts = lax.all_to_all(
        context_part.reshape(n_row, rows_c, full), ROW, split_axis=0, concat_axis=0
    )

    resid_halves = resid.reshape(n_z * 2, 2, rows_i, block_c)
    to_dot = (((2,), (0,)), ((), ()))
    away = lax.dot_general(pick(resid_halves, 1 - core, 1), context_all, to_dot, preferred_element_type=F32)
    came = lax.ppermute(away, "c", SWAP)
    home = lax.dot_general(pick(resid_halves, core, 1), context_all, to_dot, preferred_element_type=F32)
    half = (home + came).reshape(n_z, 2, rows_i, full)
    came = lax.ppermute(pick(half, 1 - xl, 1).astype(BF16), "xl", SWAP)
    quarter = pick(half, xl, 1) + came.astype(F32)
    item_parts = lax.all_to_all(quarter.astype(BF16), "z", split_axis=0, concat_axis=0)

    item_scale = 1.0 / math.sqrt(block_c * lax.axis_size(COL))
    context_scale = 1.0 / math.sqrt(block_i * n_row)
    context_sum = jnp.sum(context_parts.astype(F32), axis=0) * context_scale
    context_new, context_hist_new = adagrad(context_vec, context_hist, context_sum[:, :width])
    context_bias_new = context_bias - 0.1 * context_sum[:, width + 1]
    item_sum = jnp.sum(item_parts.astype(F32), axis=0) * item_scale
    item_new, item_hist_new = adagrad(item_vec, item_hist, item_sum[:, :width])
    item_bias_new = item_bias - 0.1 * item_sum[:, width]
    return (item_new, item_bias_new, item_hist_new, context_new, context_bias_new, context_hist_new)


def solution(mesh):
    fine = Mesh(mesh.devices.reshape(SUB_SIZES), SUB_AXES)
    by_row = ROW + COL
    by_col = COL + ROW
    return jax.shard_map(
        shards,
        mesh=fine,
        in_specs=(
            P(ROW, COL),
            P(by_row, None),
            P(by_row),
            P(by_row, None),
            P(by_col, None),
            P(by_col),
            P(by_col, None),
        ),
        out_specs=(
            P(by_row, None),
            P(by_row),
            P(by_row, None),
            P(by_col, None),
            P(by_col),
            P(by_col, None),
        ),
        check_vma=False,
    )
```

```python
import functools
import math

import jax
import jax.numpy as jnp
from jax import lax
from jax.experimental import pallas as pl
from jax.experimental.pallas import tpu as pltpu
from jax.sharding import Mesh, PartitionSpec as P

SUB_AXES = ("y", "xh", "z", "xl", "c")
SUB_SIZES = (8, 2, 12, 2, 2)
ROW = ("y", "xh")
COL = ("z", "xl", "c")
SWAP = [(0, 1), (1, 0)]
BF16 = jnp.bfloat16
F32 = jnp.float32
PAD = 128


VMEM = pl.BlockSpec(memory_space=pltpu.VMEM)
SMEM = pl.BlockSpec(memory_space=pltpu.SMEM)
PARAMS = pltpu.CompilerParams(vmem_limit_bytes=40 * 2**20)


def pick(array, index, axis):
    return lax.dynamic_index_in_dim(array, index, axis, keepdims=False)


def diagonal(n):
    return lax.broadcasted_iota(jnp.int32, (n, n), 0) == lax.broadcasted_iota(jnp.int32, (n, n), 1)


def as_column(row):
    n = row.shape[1]
    return jnp.sum(jnp.where(diagonal(n), jnp.broadcast_to(row, (n, n)), 0.0), axis=1, keepdims=True)


def as_row(column):
    n = column.shape[0]
    return jnp.sum(jnp.where(diagonal(n), jnp.broadcast_to(column, (n, n)), 0.0), axis=0, keepdims=True)


def pack_kernel(vec_ref, bias_ref, item_out, context_out):
    def tail(bias, bias_lane):
        lane = lax.broadcasted_iota(jnp.int32, (bias.shape[0], PAD), 1)
        extra = jnp.where(lane == bias_lane, bias, jnp.where(lane == 1 - bias_lane, 1.0, 0.0))
        return extra.astype(BF16)

    width = vec_ref.shape[1]
    rows_i = item_out.shape[0]
    bias = as_column(bias_ref[...])
    item_out[:, :width] = vec_ref[:rows_i].astype(BF16)
    item_out[:, width:] = tail(bias[:rows_i], 0)
    vec = vec_ref[rows_i:].astype(BF16)
    extra = tail(bias[rows_i:], 1)
    for copy in range(context_out.shape[0]):
        context_out[copy, :, :width] = vec
        context_out[copy, :, width:] = extra


def pair_kernel(where_ref, mine_ref, other_ref, out_ref):
    out_ref[where_ref[0]] = mine_ref[...]
    out_ref[1 - where_ref[0]] = other_ref[...]


def block_kernel(where_ref, counts_ref, item_ref, context_ref, away_ref, home_ref, send_ref, keep_ref, part_ref):
    core, xh = where_ref[0], where_ref[1]
    n_z, _, _, rows_i, full = item_ref.shape
    rows = n_z * 2 * rows_i
    block_c = context_ref.shape[0]
    for half, out_ref in enumerate((away_ref, home_ref)):
        c = core if half else 1 - core
        items = item_ref[:, c].reshape(rows, full)
        count = counts_ref[:, :, c].reshape(rows, block_c).astype(F32)
        contexts = context_ref[...]
        scores = lax.dot_general(items, contexts, (((1,), (1,)), ((), ())), preferred_element_type=F32)
        floor = jnp.maximum(count, 1.0)
        scaled = floor * 0.01
        power = scaled * lax.rsqrt(scaled * lax.rsqrt(scaled))
        weight = jnp.where(count > 0.0, jnp.minimum(power, 1.0), 0.0)
        resid = (weight * (scores - jnp.log(floor))).astype(BF16)
        out_ref[...] = jnp.dot(resid, contexts, preferred_element_type=F32).reshape(out_ref.shape)
        part = lax.dot_general(resid, items, (((0,), (0,)), ((), ())), preferred_element_type=F32)
        part = part.reshape(part_ref.shape)
        if half:
            part_ref[...] += part
        else:
            part_ref[...] = part
    send_ref[...] = part_ref[:, 1 - xh].astype(BF16)
    keep_ref[...] = part_ref[:, xh]


def update_kernel(scale, bias_lane, parts_ref, vec_ref, bias_ref, hist_ref, vec_out, bias_out, hist_out):
    width = vec_ref.shape[1]
    grad = jnp.sum(parts_ref[...].astype(F32), axis=0) * scale
    emb = grad[:, :width]
    hist = hist_ref[...] + emb * emb
    hist_out[...] = hist
    vec_out[...] = vec_ref[...] - 0.2 * emb / jnp.sqrt(hist)
    lane = lax.broadcasted_iota(jnp.int32, (grad.shape[0], PAD), 1)
    column = jnp.sum(jnp.where(lane == bias_lane, grad[:, width:], 0.0), axis=1, keepdims=True)
    bias_out[...] = bias_ref[...] - 0.1 * as_row(column)


def update(scale, bias_lane, parts, vec, bias, hist):
    rows = vec.shape[0]
    out = pl.pallas_call(
        functools.partial(update_kernel, scale, bias_lane),
        out_shape=(
            jax.ShapeDtypeStruct(vec.shape, F32),
            jax.ShapeDtypeStruct((1, rows), F32),
            jax.ShapeDtypeStruct(vec.shape, F32),
        ),
        in_specs=[VMEM] * 4,
        out_specs=(VMEM,) * 3,
        compiler_params=PARAMS,
    )(parts, vec, bias.reshape(1, rows), hist)
    return out[0], out[1].reshape(rows), out[2]


def shards(counts, item_vec, item_bias, item_hist, context_vec, context_bias, context_hist):
    y = lax.axis_index("y")
    xh = lax.axis_index("xh")
    xl = lax.axis_index("xl")
    core = lax.axis_index("c")
    rows_i, width = item_vec.shape
    rows_c = context_vec.shape[0]
    n_row = lax.axis_size(ROW)
    n_z = lax.axis_size("z")
    block_i, block_c = counts.shape
    full = width + PAD

    item_pack, context_copies = pl.pallas_call(
        pack_kernel,
        out_shape=(
            jax.ShapeDtypeStruct((rows_i, full), BF16),
            jax.ShapeDtypeStruct((n_row, rows_c, full), BF16),
        ),
        in_specs=[VMEM] * 2,
        out_specs=(VMEM,) * 2,
        compiler_params=PARAMS,
    )(
        jnp.concatenate([item_vec, context_vec]),
        jnp.concatenate([item_bias, context_bias]).reshape(1, rows_i + rows_c),
    )
    item_other = lax.ppermute(item_pack, "xl", SWAP)
    item_pair = pl.pallas_call(
        pair_kernel,
        out_shape=jax.ShapeDtypeStruct((2, rows_i, full), BF16),
        in_specs=[SMEM] + [VMEM] * 2,
        out_specs=VMEM,
        compiler_params=PARAMS,
    )(xl[None], item_pack, item_other)
    context_all = lax.all_to_all(context_copies, ROW, split_axis=0, concat_axis=0).reshape(block_c, full)
    item_all = lax.all_gather(item_pair, ("z", "c"), axis=0, tiled=False).reshape(n_z, 2, 2, rows_i, full)

    n_y = n_row // 2
    away, home, send, keep = pl.pallas_call(
        block_kernel,
        out_shape=(
            jax.ShapeDtypeStruct((n_z * 2, rows_i, full), F32),
            jax.ShapeDtypeStruct((n_z * 2, rows_i, full), F32),
            jax.ShapeDtypeStruct((n_y, rows_c, full), BF16),
            jax.ShapeDtypeStruct((n_y, rows_c, full), F32),
        ),
        in_specs=[SMEM] + [VMEM] * 3,
        out_specs=(VMEM,) * 4,
        scratch_shapes=[pltpu.VMEM((n_y, 2, rows_c, full), F32)],
        compiler_params=PARAMS,
    )(
        jnp.stack([core, xh]),
        counts.reshape(n_z, 2, 2, rows_i, block_c),
        item_all,
        context_all,
    )

    came = lax.ppermute(away, "c", SWAP)
    item_parts = lax.all_to_all((home + came).astype(BF16), ("z", "xl"), split_axis=0, concat_axis=0)

    came = lax.ppermute(send, "xh", SWAP)
    part = (keep + came.astype(F32)).reshape(2, 4, rows_c, full)
    total = pick(part, y % 4, 1)
    for step in (1, 2, 3):
        pairs = [(j, j ^ step) for j in range(n_y)]
        total = total + lax.ppermute(pick(part, (y % 4) ^ step, 1).astype(BF16), "y", pairs).astype(F32)
    came = lax.ppermute(pick(total, 1 - y // 4, 0).astype(BF16), "y", [(j, j ^ 4) for j in range(n_y)])
    context_parts = jnp.stack([pick(total, y // 4, 0), came.astype(F32)])

    item_scale = 1.0 / math.sqrt(block_c * lax.axis_size(COL))
    context_scale = 1.0 / math.sqrt(block_i * n_row)
    context_new, context_bias_new, context_hist_new = update(
        context_scale, 1, context_parts, context_vec, context_bias, context_hist
    )
    item_new, item_bias_new, item_hist_new = update(item_scale, 0, item_parts, item_vec, item_bias, item_hist)
    return (item_new, item_bias_new, item_hist_new, context_new, context_bias_new, context_hist_new)


def solution(mesh):
    fine = Mesh(mesh.devices.reshape(SUB_SIZES), SUB_AXES)
    by_row = ROW + COL
    by_col = COL + ROW
    return jax.shard_map(
        shards,
        mesh=fine,
        in_specs=(
            P(ROW, COL),
            P(by_row, None),
            P(by_row),
            P(by_row, None),
            P(by_col, None),
            P(by_col),
            P(by_col, None),
        ),
        out_specs=(
            P(by_row, None),
            P(by_row),
            P(by_row, None),
            P(by_col, None),
            P(by_col),
            P(by_col, None),
        ),
        check_vma=False,
    )
```

```python
import functools
import math

import jax
import jax.numpy as jnp
from jax import lax
from jax.experimental import pallas as pl
from jax.experimental.pallas import tpu as pltpu
from jax.sharding import Mesh, PartitionSpec as P

SUB_AXES = ("y", "xh", "z", "xl", "c")
SUB_SIZES = (8, 2, 12, 2, 2)
ROW = ("y", "xh")
COL = ("z", "xl", "c")
SWAP = [(0, 1), (1, 0)]
BF16 = jnp.bfloat16
F32 = jnp.float32
PAD = 128


VMEM = pl.BlockSpec(memory_space=pltpu.VMEM)
SMEM = pl.BlockSpec(memory_space=pltpu.SMEM)
PARAMS = pltpu.CompilerParams(vmem_limit_bytes=40 * 2**20)


def pick(array, index, axis):
    return lax.dynamic_index_in_dim(array, index, axis, keepdims=False)


def diagonal(n):
    return lax.broadcasted_iota(jnp.int32, (n, n), 0) == lax.broadcasted_iota(jnp.int32, (n, n), 1)


def as_column(row):
    n = row.shape[1]
    return jnp.sum(jnp.where(diagonal(n), jnp.broadcast_to(row, (n, n)), 0.0), axis=1, keepdims=True)


def as_row(column):
    n = column.shape[0]
    return jnp.sum(jnp.where(diagonal(n), jnp.broadcast_to(column, (n, n)), 0.0), axis=0, keepdims=True)


def pack_kernel(vec_ref, item_out, context_out):
    def tail(bias, bias_lane):
        lane = lax.broadcasted_iota(jnp.int32, (bias.shape[0], PAD), 1)
        extra = jnp.where(lane == bias_lane, bias, jnp.where(lane == 1 - bias_lane, 1.0, 0.0))
        return extra.astype(BF16)

    width = vec_ref.shape[1]
    rows_i = item_out.shape[0]
    rows = rows_i + context_out.shape[1]
    bias = as_column(vec_ref[rows:, :rows])
    item_out[:, :width] = vec_ref[:rows_i].astype(BF16)
    item_out[:, width:] = tail(bias[:rows_i], 0)
    vec = vec_ref[rows_i:rows].astype(BF16)
    extra = tail(bias[rows_i:], 1)
    for copy in range(context_out.shape[0]):
        context_out[copy, :, :width] = vec
        context_out[copy, :, width:] = extra


def block_kernel(where_ref, counts_ref, item_ref, context_ref, away_ref, home_ref, send_ref, keep_ref, part_ref):
    core, xh = where_ref[0], where_ref[1]
    n_z, _, _, rows_i, full = item_ref.shape
    rows = n_z * 2 * rows_i
    block_c = context_ref.shape[0]
    for half, out_ref in enumerate((away_ref, home_ref)):
        c = core if half else 1 - core
        items = item_ref[:, c].reshape(rows, full)
        count = counts_ref[:, :, c].reshape(rows, block_c).astype(F32)
        contexts = context_ref[...]
        scores = lax.dot_general(items, contexts, (((1,), (1,)), ((), ())), preferred_element_type=F32)
        floor = jnp.maximum(count, 1.0)
        scaled = floor * 0.01
        power = scaled * lax.rsqrt(scaled * lax.rsqrt(scaled))
        weight = jnp.where(count > 0.0, jnp.minimum(power, 1.0), 0.0)
        resid = (weight * (scores - jnp.log(floor))).astype(BF16)
        out_ref[...] = jnp.dot(resid, contexts, preferred_element_type=F32).reshape(out_ref.shape)
        part = lax.dot_general(resid, items, (((0,), (0,)), ((), ())), preferred_element_type=F32)
        part = part.reshape(part_ref.shape)
        if half:
            part_ref[...] += part
        else:
            part_ref[...] = part
    send_ref[...] = part_ref[:, 1 - xh].astype(BF16)
    keep_ref[...] = part_ref[:, xh]


def update_kernel(scale, bias_lane, parts_ref, vec_ref, bias_ref, hist_ref, vec_out, bias_out, hist_out):
    width = vec_ref.shape[1]
    grad = jnp.sum(parts_ref[...].astype(F32), axis=0) * scale
    emb = grad[:, :width]
    hist = hist_ref[...] + emb * emb
    hist_out[...] = hist
    vec_out[...] = vec_ref[...] - 0.2 * emb / jnp.sqrt(hist)
    lane = lax.broadcasted_iota(jnp.int32, (grad.shape[0], PAD), 1)
    column = jnp.sum(jnp.where(lane == bias_lane, grad[:, width:], 0.0), axis=1, keepdims=True)
    bias_out[...] = bias_ref[...] - 0.1 * as_row(column)


def update(scale, bias_lane, parts, vec, bias, hist):
    rows = vec.shape[0]
    out = pl.pallas_call(
        functools.partial(update_kernel, scale, bias_lane),
        out_shape=(
            jax.ShapeDtypeStruct(vec.shape, F32),
            jax.ShapeDtypeStruct((1, rows), F32),
            jax.ShapeDtypeStruct(vec.shape, F32),
        ),
        in_specs=[VMEM] * 4,
        out_specs=(VMEM,) * 3,
        compiler_params=PARAMS,
    )(parts, vec, bias.reshape(1, rows), hist)
    return out[0], out[1].reshape(rows), out[2]


def shards(counts, item_vec, item_bias, item_hist, context_vec, context_bias, context_hist):
    y = lax.axis_index("y")
    xh = lax.axis_index("xh")
    core = lax.axis_index("c")
    rows_i, width = item_vec.shape
    rows_c = context_vec.shape[0]
    n_row = lax.axis_size(ROW)
    n_z = lax.axis_size("z")
    block_i, block_c = counts.shape
    full = width + PAD

    biases = jnp.concatenate([item_bias, context_bias])
    bias_row = jnp.pad(biases, (0, width - biases.shape[0]))
    item_pack, context_copies = pl.pallas_call(
        pack_kernel,
        out_shape=(
            jax.ShapeDtypeStruct((rows_i, full), BF16),
            jax.ShapeDtypeStruct((n_row, rows_c, full), BF16),
        ),
        in_specs=[VMEM],
        out_specs=(VMEM,) * 2,
        compiler_params=PARAMS,
    )(jnp.concatenate([item_vec, context_vec, bias_row[None]]))
    context_all = lax.all_to_all(context_copies, ROW, split_axis=0, concat_axis=0).reshape(block_c, full)
    item_pair = lax.all_gather(item_pack, "xl", axis=0, tiled=False)
    item_all = lax.all_gather(item_pair, ("z", "c"), axis=0, tiled=False).reshape(n_z, 2, 2, rows_i, full)

    n_y = n_row // 2
    away, home, send, keep = pl.pallas_call(
        block_kernel,
        out_shape=(
            jax.ShapeDtypeStruct((n_z * 2, rows_i, full), F32),
            jax.ShapeDtypeStruct((n_z * 2, rows_i, full), F32),
            jax.ShapeDtypeStruct((n_y, rows_c, full), BF16),
            jax.ShapeDtypeStruct((n_y, rows_c, full), F32),
        ),
        in_specs=[SMEM] + [VMEM] * 3,
        out_specs=(VMEM, VMEM, VMEM, VMEM),
        scratch_shapes=[pltpu.VMEM((n_y, 2, rows_c, full), F32)],
        compiler_params=PARAMS,
    )(
        jnp.stack([core, xh]),
        counts.reshape(n_z, 2, 2, rows_i, block_c),
        item_all,
        context_all,
    )

    came = lax.ppermute(away, "c", SWAP)
    item_parts = lax.all_to_all((home + came).astype(BF16), ("z", "xl"), split_axis=0, concat_axis=0)

    came = lax.ppermute(send, "xh", SWAP)
    part = (keep + came.astype(F32)).reshape(2, 4, rows_c, full)
    total = pick(part, y % 4, 1)
    for step in (1, 2, 3):
        pairs = [(j, j ^ step) for j in range(n_y)]
        total = total + lax.ppermute(pick(part, (y % 4) ^ step, 1).astype(BF16), "y", pairs).astype(F32)
    came = lax.ppermute(pick(total, 1 - y // 4, 0).astype(BF16), "y", [(j, j ^ 4) for j in range(n_y)])
    context_parts = jnp.stack([pick(total, y // 4, 0), came.astype(F32)])

    item_scale = 1.0 / math.sqrt(block_c * lax.axis_size(COL))
    context_scale = 1.0 / math.sqrt(block_i * n_row)
    context_new, context_bias_new, context_hist_new = update(
        context_scale, 1, context_parts, context_vec, context_bias, context_hist
    )
    item_new, item_bias_new, item_hist_new = update(item_scale, 0, item_parts, item_vec, item_bias, item_hist)
    return (item_new, item_bias_new, item_hist_new, context_new, context_bias_new, context_hist_new)


def solution(mesh):
    fine = Mesh(mesh.devices.reshape(SUB_SIZES), SUB_AXES)
    by_row = ROW + COL
    by_col = COL + ROW
    return jax.shard_map(
        shards,
        mesh=fine,
        in_specs=(
            P(ROW, COL),
            P(by_row, None),
            P(by_row),
            P(by_row, None),
            P(by_col, None),
            P(by_col),
            P(by_col, None),
        ),
        out_specs=(
            P(by_row, None),
            P(by_row),
            P(by_row, None),
            P(by_col, None),
            P(by_col),
            P(by_col, None),
        ),
        check_vma=False,
    )
```

```python
import functools
import math

import jax
import jax.numpy as jnp
from jax import lax
from jax.experimental import pallas as pl
from jax.experimental.pallas import tpu as pltpu
from jax.sharding import Mesh, PartitionSpec as P

SUB_AXES = ("y", "xh", "z", "xl", "c")
SUB_SIZES = (8, 2, 12, 2, 2)
ROW = ("y", "xh")
COL = ("z", "xl", "c")
SWAP = [(0, 1), (1, 0)]
BF16 = jnp.bfloat16
F32 = jnp.float32
PAD = 128


VMEM = pl.BlockSpec(memory_space=pltpu.VMEM)
SMEM = pl.BlockSpec(memory_space=pltpu.SMEM)
PARAMS = pltpu.CompilerParams(vmem_limit_bytes=40 * 2**20)


def pick(array, index, axis):
    return lax.dynamic_index_in_dim(array, index, axis, keepdims=False)


def diagonal(n):
    return lax.broadcasted_iota(jnp.int32, (n, n), 0) == lax.broadcasted_iota(jnp.int32, (n, n), 1)


def as_column(row):
    n = row.shape[1]
    return jnp.sum(jnp.where(diagonal(n), jnp.broadcast_to(row, (n, n)), 0.0), axis=1, keepdims=True)


def as_row(column):
    n = column.shape[0]
    return jnp.sum(jnp.where(diagonal(n), jnp.broadcast_to(column, (n, n)), 0.0), axis=0, keepdims=True)


def pack_kernel(vec_ref, item_out, context_out):
    def tail(bias, bias_lane):
        lane = lax.broadcasted_iota(jnp.int32, (bias.shape[0], PAD), 1)
        extra = jnp.where(lane == bias_lane, bias, jnp.where(lane == 1 - bias_lane, 1.0, 0.0))
        return extra.astype(BF16)

    width = vec_ref.shape[1]
    rows_i = item_out.shape[0]
    rows = rows_i + context_out.shape[1]
    bias = as_column(vec_ref[rows:, :rows])
    item_out[:, :width] = vec_ref[:rows_i].astype(BF16)
    item_out[:, width:] = tail(bias[:rows_i], 0)
    vec = vec_ref[rows_i:rows].astype(BF16)
    extra = tail(bias[rows_i:], 1)
    for copy in range(context_out.shape[0]):
        context_out[copy, :, :width] = vec
        context_out[copy, :, width:] = extra


def block_kernel(where_ref, counts_ref, item_ref, context_ref, away_ref, home_ref, send_ref, keep_ref, part_ref):
    core, xh = where_ref[0], where_ref[1]
    n_z, _, _, rows_i, full = item_ref.shape
    rows = n_z * 2 * rows_i
    block_c = context_ref.shape[0]
    for half, out_ref in enumerate((away_ref, home_ref)):
        c = core if half else 1 - core
        items = item_ref[:, c].reshape(rows, full)
        count = counts_ref[:, :, c].reshape(rows, block_c).astype(F32)
        contexts = context_ref[...]
        scores = lax.dot_general(items, contexts, (((1,), (1,)), ((), ())), preferred_element_type=F32)
        floor = jnp.maximum(count, 1.0)
        scaled = floor * 0.01
        power = scaled * lax.rsqrt(scaled * lax.rsqrt(scaled))
        weight = jnp.where(count > 0.0, jnp.minimum(power, 1.0), 0.0)
        resid = (weight * (scores - jnp.log(floor))).astype(BF16)
        out = jnp.dot(resid, contexts, preferred_element_type=F32)
        out_ref[...] = out.reshape(out_ref.shape).astype(out_ref.dtype)
        part = lax.dot_general(resid, items, (((0,), (0,)), ((), ())), preferred_element_type=F32)
        part = part.reshape(part_ref.shape)
        if half:
            part_ref[...] += part
        else:
            part_ref[...] = part
    send_ref[...] = part_ref[:, 1 - xh].astype(BF16)
    keep_ref[...] = part_ref[:, xh]


def update_kernel(scale, bias_lane, parts_ref, vec_ref, bias_ref, hist_ref, vec_out, bias_out, hist_out):
    width = vec_ref.shape[1]
    grad = jnp.sum(parts_ref[...].astype(F32), axis=0) * scale
    emb = grad[:, :width]
    hist = hist_ref[...] + emb * emb
    hist_out[...] = hist
    vec_out[...] = vec_ref[...] - 0.2 * emb / jnp.sqrt(hist)
    lane = lax.broadcasted_iota(jnp.int32, (grad.shape[0], PAD), 1)
    column = jnp.sum(jnp.where(lane == bias_lane, grad[:, width:], 0.0), axis=1, keepdims=True)
    bias_out[...] = bias_ref[...] - 0.1 * as_row(column)


def update(scale, bias_lane, parts, vec, bias, hist):
    rows = vec.shape[0]
    out = pl.pallas_call(
        functools.partial(update_kernel, scale, bias_lane),
        out_shape=(
            jax.ShapeDtypeStruct(vec.shape, F32),
            jax.ShapeDtypeStruct((1, rows), F32),
            jax.ShapeDtypeStruct(vec.shape, F32),
        ),
        in_specs=[VMEM] * 4,
        out_specs=(VMEM,) * 3,
        compiler_params=PARAMS,
    )(parts, vec, bias.reshape(1, rows), hist)
    return out[0], out[1].reshape(rows), out[2]


def shards(counts, item_vec, item_bias, item_hist, context_vec, context_bias, context_hist):
    y = lax.axis_index("y")
    xh = lax.axis_index("xh")
    core = lax.axis_index("c")
    rows_i, width = item_vec.shape
    rows_c = context_vec.shape[0]
    n_row = lax.axis_size(ROW)
    n_z = lax.axis_size("z")
    block_i, block_c = counts.shape
    full = width + PAD

    biases = jnp.concatenate([item_bias, context_bias])
    bias_row = jnp.pad(biases, (0, width - biases.shape[0]))
    item_pack, context_copies = pl.pallas_call(
        pack_kernel,
        out_shape=(
            jax.ShapeDtypeStruct((rows_i, full), BF16),
            jax.ShapeDtypeStruct((n_row, rows_c, full), BF16),
        ),
        in_specs=[VMEM],
        out_specs=(VMEM,) * 2,
        compiler_params=PARAMS,
    )(jnp.concatenate([item_vec, context_vec, bias_row[None]]))
    context_all = lax.all_to_all(context_copies, ROW, split_axis=0, concat_axis=0).reshape(block_c, full)
    item_pair = lax.all_gather(item_pack, "xl", axis=0, tiled=False)
    item_all = lax.all_gather(item_pair, ("z", "c"), axis=0, tiled=False).reshape(n_z, 2, 2, rows_i, full)

    n_y = n_row // 2
    away, home, send, keep = pl.pallas_call(
        block_kernel,
        out_shape=(
            jax.ShapeDtypeStruct((n_z * 2, rows_i, full), BF16),
            jax.ShapeDtypeStruct((n_z * 2, rows_i, full), F32),
            jax.ShapeDtypeStruct((n_y, rows_c, full), BF16),
            jax.ShapeDtypeStruct((n_y, rows_c, full), F32),
        ),
        in_specs=[SMEM] + [VMEM] * 3,
        out_specs=(VMEM, VMEM, VMEM, VMEM),
        scratch_shapes=[pltpu.VMEM((n_y, 2, rows_c, full), F32)],
        compiler_params=PARAMS,
    )(
        jnp.stack([core, xh]),
        counts.reshape(n_z, 2, 2, rows_i, block_c),
        item_all,
        context_all,
    )

    came = lax.ppermute(away, "c", SWAP)
    item_parts = lax.all_to_all((home + came.astype(F32)).astype(BF16), ("z", "xl"), split_axis=0, concat_axis=0)

    came = lax.ppermute(send, "xh", SWAP)
    part = (keep + came.astype(F32)).reshape(2, 4, rows_c, full)
    total = pick(part, y % 4, 1)
    for step in (1, 2, 3):
        pairs = [(j, j ^ step) for j in range(n_y)]
        total = total + lax.ppermute(pick(part, (y % 4) ^ step, 1).astype(BF16), "y", pairs).astype(F32)
    came = lax.ppermute(pick(total, 1 - y // 4, 0).astype(BF16), "y", [(j, j ^ 4) for j in range(n_y)])
    context_parts = jnp.stack([pick(total, y // 4, 0), came.astype(F32)])

    item_scale = 1.0 / math.sqrt(block_c * lax.axis_size(COL))
    context_scale = 1.0 / math.sqrt(block_i * n_row)
    context_new, context_bias_new, context_hist_new = update(
        context_scale, 1, context_parts, context_vec, context_bias, context_hist
    )
    item_new, item_bias_new, item_hist_new = update(item_scale, 0, item_parts, item_vec, item_bias, item_hist)
    return (item_new, item_bias_new, item_hist_new, context_new, context_bias_new, context_hist_new)


def solution(mesh):
    fine = Mesh(mesh.devices.reshape(SUB_SIZES), SUB_AXES)
    by_row = ROW + COL
    by_col = COL + ROW
    return jax.shard_map(
        shards,
        mesh=fine,
        in_specs=(
            P(ROW, COL),
            P(by_row, None),
            P(by_row),
            P(by_row, None),
            P(by_col, None),
            P(by_col),
            P(by_col, None),
        ),
        out_specs=(
            P(by_row, None),
            P(by_row),
            P(by_row, None),
            P(by_col, None),
            P(by_col),
            P(by_col, None),
        ),
        check_vma=False,
    )
```
